512 devices in a mesh: seq: 32 (over z, core), head: 16 (over y, x).
Axes of the slice: x: 4, y: 4, z: 16, core: 2. Of those that a mesh axis runs over, the one named last changes fastest.
Arguments:
- query_in: bfloat16 [65536, 2048], P(('seq', 'head')), may hold values from -4.6 to 4.6
- key_in: bfloat16 [65536, 2048], P(('seq', 'head')), may hold values from -4.6 to 4.6
- value_in: bfloat16 [65536, 2048], P(('seq', 'head')), may hold values from -6 to 6
- grad_out: bfloat16 [65536, 2048], P(('seq', 'head')), may hold values from -6 to 6
- module_lengths: int32 [512], replicated, may hold values from 1 to 256, 65536 in all
Outputs:
- attn_out: bfloat16 [65536, 2048], P(('seq', 'head'))
- grad_query: bfloat16 [65536, 2048], P(('seq', 'head'))
- grad_key: bfloat16 [65536, 2048], P(('seq', 'head'))
- grad_value: bfloat16 [65536, 2048], P(('seq', 'head'))
The draws below stay inside these ranges and needn't reach their ends.
Inputs may be any that keep to these rules, and one draw needn't show every extreme that they name: `module_lengths`: the lengths sum to 65536; the longest is exactly 256.
All inputs are finite; a program needn't handle non-finite values.
Results may differ from the reference program's by a relative error of at most 0.03.
Values may be sent and summed in bfloat16 or wider, within the bound.
A program may use at most 64 MiB of HBM per device.

```python
import math
import jax
import jax.numpy as jnp
import numpy as np
from jax import lax

HEADS = 16
HEAD_DIM = 128
D = 2048
TOK_DEV = 128
PRIOR = 256
TOKENS = 65536
MODULES = 512
N_SEQ = 32
N_HEAD = 16


def drawn_rows(key, role_code):
    result = jnp.clip(jax.random.normal(jax.random.fold_in(key, role_code), (TOKENS, D), jnp.float32), -4.6, 4.6)
    return result.astype(jnp.bfloat16)


def draw_query_in(key, part):
    return drawn_rows(key, 1)


def draw_key_in(key, part):
    return drawn_rows(key, 2)


def shard_levels(stream_key, extent, shards, least, largest):
    loudness, own = 1.0, jax.random.fold_in(stream_key, 6)
    for axis_at, blocks in shards:
        steps = jnp.exp(jax.random.uniform(jax.random.fold_in(own, axis_at), (blocks,), jnp.float32, least / len(shards), largest / len(shards)))
        loudness = loudness * jnp.repeat(steps, extent[axis_at] // blocks).reshape([-1 if axis == axis_at else 1 for axis in range(len(extent))])
    return loudness


def length_profile(number_of, total, bound, lean):
    portions = [(1 << 20) // math.isqrt(standing ** lean) + 1 for standing in range(2, number_of + 1)]
    rest, given = total - bound - (number_of - 1), [1] * (number_of - 1)
    while rest > 0:
        movable = [i for i in range(number_of - 1) if given[i] < bound]
        whole, remaining = sum([portions[i] for i in movable]), rest
        for i in movable:
            more = min(bound - given[i], max(1, remaining * portions[i] // whole), rest)
            given[i] = given[i] + more
            rest = rest - more
    return np.array([bound] + given)


def uneven_parts(own_key, count, total, reach, slope):
    if count == 2:
        one = jax.random.randint(own_key, (), max(1, total - reach), min(reach, total - 1) + 1)
        return jnp.stack([one, total - one])
    sizes = jnp.asarray(length_profile(count, total, reach, slope), jnp.int32)
    pairs = (count - 1) // 2
    source_of, receiver = sizes[1:1 + 2 * pairs:2], sizes[2:2 + 2 * pairs:2]
    room = jnp.minimum(source_of - 1, reach - receiver)
    moved = jax.random.randint(jax.random.fold_in(own_key, 1), (pairs,), 0, 1 << 20) % (room + 1)
    sizes = sizes.at[1:1 + 2 * pairs:2].set(source_of - moved).at[2:2 + 2 * pairs:2].set(receiver + moved)
    return sizes[jax.random.permutation(jax.random.fold_in(own_key, 2), count)]


def noise(key, extent, spread, most, pieces=(), kind=jnp.bfloat16):
    factor_of = shard_levels(key, extent, pieces, -0.22, 0.18) if pieces else 1.0
    values = jax.random.normal(key, extent, jnp.float32) * spread * factor_of
    return jnp.minimum(jnp.maximum(values, -most), most).astype(kind)


def setup_inputs(seed: int = 0) -> dict:
    splits = jax.random.split(jax.random.key(seed), 6)
    query_in = draw_query_in(jax.random.fold_in(splits[5], 71), 0)
    key_in = draw_key_in(jax.random.fold_in(splits[5], 71), 0)
    value_in = noise(splits[2], (TOKENS, D), 1.0, 6.0, ((0, 512),))
    grad_out = noise(splits[3], (TOKENS, D), 1.0, 6.0, ((0, 512),))
    module_lengths = uneven_parts(splits[4], MODULES, TOKENS, PRIOR, 2).astype(jnp.int32)
    return dict(query_in=query_in, key_in=key_in, value_in=value_in, grad_out=grad_out, module_lengths=module_lengths)


def module_ids(module_lengths, positions):
    module_ends = jnp.cumsum(module_lengths)
    counted = jnp.sum((positions[:, None] >= module_ends[None, :]).astype(jnp.int32), axis=1).astype(jnp.int32)
    return jnp.where(positions >= 0, counted, -1)


def allowed_pairs(module_lengths, query_pos, key_pos):
    same = module_ids(module_lengths, query_pos)[:, None] == module_ids(module_lengths, key_pos)[None, :]
    return same & (key_pos[None, :] <= query_pos[:, None])


def attend_block(query_rows, key_block, value_block, grad_rows, allowed, score_scale):
    high = lax.Precision.HIGHEST
    query_f = query_rows.astype(jnp.float32)
    key_f = key_block.astype(jnp.float32)
    value_f = value_block.astype(jnp.float32)
    grad_f = grad_rows.astype(jnp.float32)
    scores = jnp.einsum('qhd,khd->hqk', query_f, key_f, precision=high) * score_scale
    allowed_mask = allowed[None]
    row_top = jnp.max(jnp.where(allowed_mask, scores, -jnp.inf), axis=2, keepdims=True)
    row_total = jnp.sum(jnp.where(allowed_mask, jnp.exp(scores - row_top), 0.0), axis=2, keepdims=True)
    log_total = row_top + jnp.log(row_total)
    weights = jnp.where(allowed_mask, jnp.exp(scores - log_total), 0.0)
    weight_bf = weights.astype(jnp.bfloat16)
    attn_rows = jnp.einsum('hqk,khd->qhd', weight_bf.astype(jnp.float32), value_f, precision=high).astype(jnp.bfloat16)
    row_delta = jnp.transpose(jnp.sum(grad_f * attn_rows.astype(jnp.float32), axis=2))
    dprobs = jnp.einsum('qhd,khd->hqk', grad_f, value_f, precision=high)
    dscores = (weights * (dprobs - row_delta[:, :, None]) * score_scale).astype(jnp.bfloat16)
    dscores_f = dscores.astype(jnp.float32)
    grad_q = jnp.einsum('hqk,khd->qhd', dscores_f, key_f, precision=high).astype(jnp.bfloat16)
    key_grad = jnp.einsum('hqk,qhd->khd', dscores_f, query_f, precision=high)
    value_grad = jnp.einsum('hqk,qhd->khd', weight_bf.astype(jnp.float32), grad_f, precision=high)
    return attn_rows, grad_q, key_grad, value_grad


def reference(query_in, key_in, value_in, grad_out, module_lengths):
    row_count = TOK_DEV * N_HEAD
    prior_rows = row_count // 8
    score_scale = HEAD_DIM ** -0.5

    def to_blocks(whole):
        return whole.reshape(N_SEQ, row_count, HEADS, HEAD_DIM)

    query_b = to_blocks(query_in)
    key_b = to_blocks(key_in)
    value_b = to_blocks(value_in)
    grad_b = to_blocks(grad_out)
    zero_block = jnp.zeros((1, prior_rows, HEADS, HEAD_DIM), key_b.dtype)
    prior_k = jnp.concatenate([zero_block, key_b[:-1, row_count - prior_rows:]], axis=0)
    prior_v = jnp.concatenate([zero_block, value_b[:-1, row_count - prior_rows:]], axis=0)

    def per_block(packed):
        block_idx, query_rows, own_k, own_v, before_k, before_v, grad_rows = packed
        block_start = block_idx * row_count
        query_pos = block_start + jnp.arange(row_count, dtype=jnp.int32)
        before_pos = block_start - prior_rows + jnp.arange(prior_rows, dtype=jnp.int32)
        key_pos = jnp.concatenate([before_pos, query_pos])
        allowed = allowed_pairs(module_lengths, query_pos, key_pos)
        key_block = jnp.concatenate([before_k, own_k], axis=0)
        value_block = jnp.concatenate([before_v, own_v], axis=0)
        return attend_block(query_rows, key_block, value_block, grad_rows, allowed, score_scale)

    block_ids = jnp.arange(N_SEQ, dtype=jnp.int32)
    attn_rows, grad_q, key_grad, value_grad = lax.map(per_block, (block_ids, query_b, key_b, value_b, prior_k, prior_v, grad_b))
    zero_f = jnp.zeros((1, prior_rows, HEADS, HEAD_DIM), jnp.float32)
    later_k = jnp.concatenate([key_grad[1:, :prior_rows], zero_f], axis=0)
    later_v = jnp.concatenate([value_grad[1:, :prior_rows], zero_f], axis=0)
    key_total = key_grad[:, prior_rows:].at[:, row_count - prior_rows:].add(later_k)
    value_total = value_grad[:, prior_rows:].at[:, row_count - prior_rows:].add(later_v)
    return (attn_rows.reshape(TOKENS, D), grad_q.reshape(TOKENS, D),
            key_total.astype(jnp.bfloat16).reshape(TOKENS, D), value_total.astype(jnp.bfloat16).reshape(TOKENS, D))
```

```python
import functools

import jax
import jax.numpy as jnp
from jax import lax
from jax.experimental import pallas as pl
from jax.experimental.pallas import tpu as pltpu
from jax.sharding import PartitionSpec as P

HD = 128
ROWS = 128
NX = 4
STAGES = 4
LINE = NX * ROWS
HALO = 256
SCALE = HD ** (-0.5)
LOG2E = 1.4426950408889634
MASKED = -1e30
MESH = pl.DeviceIdType.MESH


def dot(a, b, dims):
    return lax.dot_general(a, b, (dims, ((), ())), preferred_element_type=jnp.float32)


def kernel(
    n_seq,
    n_y,
    len_ref,
    q_in,
    k_in,
    v_in,
    g_in,
    o_out,
    dq_out,
    dk_out,
    dv_out,
    qg,
    kv,
    acc,
    outs,
    part_in,
    part_out,
    start_ref,
    in_send,
    in_recv,
    own_sem,
    halo_send,
    halo_recv,
    part_send,
    part_recv,
    out_send,
    out_recv,
):
    s = lax.axis_index("seq")
    h = lax.axis_index("head")
    y, x = h // NX, h % NX
    ins = (k_in, v_in, q_in, g_in)
    results = (o_out, dq_out, dk_out, dv_out)
    wrap_next = (y + 1) // n_y
    after = ((s + wrap_next) % n_seq, ((y + 1) % n_y) * NX + x)
    wrap_prev = (n_y - y) // n_y
    before = ((s + n_seq - wrap_prev) % n_seq, ((y + n_y - 1) % n_y) * NX + x)

    def in_row(peer_x):
        return (s, y * NX + peer_x)

    def rows(at):
        return pl.ds(pl.multiple_of(at * ROWS, ROWS), ROWS)

    def cols(owner, st):
        return pl.ds(pl.multiple_of((owner * STAGES + st) * HD, HD), HD)

    def landing(st, t, from_x):
        if t < 2:
            return kv.at[st, t, rows(from_x + HALO // ROWS)]
        return qg.at[st, t - 2, rows(from_x)]

    def in_copy(st, t, d):
        to = (x + d) % NX
        return pltpu.make_async_remote_copy(
            src_ref=ins[t].at[:, cols(to, st)],
            dst_ref=landing(st, t, x),
            send_sem=in_send.at[st, t, d - 1],
            recv_sem=in_recv.at[st, t, d - 1],
            device_id=in_row(to),
            device_id_type=MESH,
        )

    def own_copy(st, t):
        return pltpu.make_async_copy(
            ins[t].at[:, cols(x, st)], landing(st, t, x), own_sem.at[st, t]
        )

    def halo_copy(st, t):
        return pltpu.make_async_remote_copy(
            src_ref=kv.at[st, t, pl.ds(LINE, HALO)],
            dst_ref=kv.at[st, t, pl.ds(0, HALO)],
            send_sem=halo_send.at[st, t],
            recv_sem=halo_recv.at[st, t],
            device_id=after,
            device_id_type=MESH,
        )

    def part_copy(st, t):
        return pltpu.make_async_remote_copy(
            src_ref=part_out.at[st, t],
            dst_ref=part_in.at[st, t],
            send_sem=part_send.at[st, t],
            recv_sem=part_recv.at[st, t],
            device_id=before,
            device_id_type=MESH,
        )

    def out_copy(st, t, to):
        return pltpu.make_async_remote_copy(
            src_ref=outs.at[st, t, pl.ds(to * ROWS, ROWS)],
            dst_ref=results[t].at[:, cols(x, st)],
            send_sem=out_send.at[st, t, to],
            recv_sem=out_recv.at[st, t, x],
            device_id=in_row(to),
            device_id_type=MESH,
        )

    def out_own(st, t, to):
        return pltpu.make_async_copy(
            outs.at[st, t, pl.ds(to * ROWS, ROWS)],
            results[t].at[:, cols(x, st)],
            out_recv.at[st, t, x],
        )

    def send_out(st, kinds, half):
        for to in (2 * half, 2 * half + 1):

            @pl.when(x != to)
            def _():
                for t in kinds:
                    out_copy(st, t, to).start()

            @pl.when(x == to)
            def _():
                for t in kinds:
                    out_own(st, t, to).start()

    barrier = pltpu.get_barrier_semaphore()
    for d in range(1, NX):
        pl.semaphore_signal(barrier, inc=1, device_id=in_row((x + d) % NX), device_id_type=MESH)
    for there in (after, before):
        pl.semaphore_signal(barrier, inc=1, device_id=there, device_id_type=MESH)
    pl.semaphore_wait(barrier, NX + 1)

    def send_in(st, carry):
        for t in range(4):
            for d in (2, 1, 3):
                in_copy(st, t, d).start()
            own_copy(st, t).start()
        return carry

    lax.fori_loop(0, STAGES, send_in, 0)

    lengths = len_ref[...].astype(jnp.float32)
    n_mod = lengths.shape[1]
    m_at = lax.broadcasted_iota(jnp.int32, (n_mod, n_mod), 0)
    l_at = lax.broadcasted_iota(jnp.int32, (n_mod, n_mod), 1)
    ends = jnp.sum(jnp.where(l_at <= m_at, lengths, 0.0), axis=1, keepdims=True)
    base = (s * n_y + y) * LINE
    token = (base + lax.broadcasted_iota(jnp.int32, (1, LINE), 1)).astype(jnp.float32)
    begun = jnp.max(jnp.where(ends <= token, ends, 0.0), axis=0, keepdims=True)
    start_ref[...] = begun.astype(jnp.int32) - base

    def block(st, half):
        q = qg[st, 0, pl.ds(half * HALO, HALO), :]
        g = qg[st, 1, pl.ds(half * HALO, HALO), :]
        k = kv[st, 0, pl.ds(half * HALO, 2 * HALO), :]
        v = kv[st, 1, pl.ds(half * HALO, 2 * HALO), :]
        first = start_ref[:, pl.ds(half * HALO, HALO)] - half * HALO
        key_at = lax.broadcasted_iota(jnp.int32, (2 * HALO, HALO), 0) - HALO
        query_at = lax.broadcasted_iota(jnp.int32, (2 * HALO, HALO), 1)
        allowed = (key_at <= query_at) & (key_at >= first)
        scores = jnp.where(allowed, dot(k, q, ((1,), (1,))) * (SCALE * LOG2E), MASKED)
        top = jnp.max(scores, axis=0, keepdims=True)
        powers = jnp.exp2(scores - top)
        weights = powers * (1.0 / jnp.sum(powers, axis=0, keepdims=True))
        weight_bf = weights.astype(jnp.bfloat16)
        dprobs = dot(v, g, ((1,), (1,)))
        delta = jnp.sum(weights * dprobs, axis=0, keepdims=True)
        dscores = (weights * (dprobs - delta)).astype(jnp.bfloat16)
        here = pl.ds(half * HALO, HALO)
        outs[st, 0, here, :] = dot(weight_bf, v, ((0,), (0,))).astype(jnp.bfloat16)
        outs[st, 1, here, :] = (dot(dscores, k, ((0,), (0,))) * SCALE).astype(jnp.bfloat16)
        dk = dot(dscores, q, ((1,), (0,))) * SCALE
        dv = dot(weight_bf, g, ((1,), (0,)))
        return dk, dv

    def finish(st):
        for t in range(2):
            part_copy(st, t).wait_recv()
            total = acc[st, t, pl.ds(HALO, HALO), :] + part_in[st, t].astype(jnp.float32)
            outs[st, 2 + t, pl.ds(HALO, HALO), :] = total.astype(jnp.bfloat16)
        send_out(st, (2, 3), 1)

    def stage(st, carry):
        for t in range(4):
            own_copy(st, t).wait()
            for d in range(1, NX):
                in_copy(st, t, d).wait_recv()
            if t < 2:
                halo_copy(st, t).start()
        for t, grad in enumerate(block(st, 1)):
            acc[st, t] = grad
        send_out(st, (0, 1), 1)

        @pl.when(st > 0)
        def _():
            finish(st - 1)

        for t in range(2):
            halo_copy(st, t).wait_recv()
        for t, grad in enumerate(block(st, 0)):
            part_out[st, t] = grad[:HALO].astype(jnp.bfloat16)
            part_copy(st, t).start()
            total = acc[st, t, pl.ds(0, HALO), :] + grad[HALO:]
            outs[st, 2 + t, pl.ds(0, HALO), :] = total.astype(jnp.bfloat16)
        send_out(st, (0, 1, 2, 3), 0)
        return carry

    lax.fori_loop(0, STAGES, stage, 0)
    finish(STAGES - 1)

    def drain(st, carry):
        for t in range(4):
            for d in range(1, NX):
                in_copy(st, t, d).wait_send()
        for t in range(2):
            halo_copy(st, t).wait_send()
            part_copy(st, t).wait_send()
        for t in range(4):
            for peer in range(NX):

                @pl.when(x != peer)
                def _():
                    out_copy(st, t, peer).wait_send()
                    pltpu.make_async_remote_copy(
                        src_ref=outs.at[st, t, pl.ds(peer * ROWS, ROWS)],
                        dst_ref=results[t].at[:, cols(peer, st)],
                        send_sem=out_send.at[st, t, peer],
                        recv_sem=out_recv.at[st, t, peer],
                        device_id=in_row(peer),
                        device_id_type=MESH,
                    ).wait_recv()

                @pl.when(x == peer)
                def _():
                    out_own(st, t, peer).wait()
        return carry

    lax.fori_loop(0, STAGES, drain, 0)


def shards(n_seq, n_y, query_in, key_in, value_in, grad_out, module_lengths):
    any_space = pl.BlockSpec(memory_space=pl.ANY)
    vmem = pl.BlockSpec(memory_space=pltpu.VMEM)
    bf16, f32 = jnp.bfloat16, jnp.float32
    sems = pltpu.SemaphoreType.DMA
    return pl.pallas_call(
        functools.partial(kernel, n_seq, n_y),
        out_shape=[jax.ShapeDtypeStruct(query_in.shape, bf16)] * 4,
        in_specs=[vmem] + [any_space] * 4,
        out_specs=[vmem] * 4,
        scratch_shapes=[
            pltpu.VMEM((STAGES, 2, LINE, HD), bf16),
            pltpu.VMEM((STAGES, 2, LINE + HALO, HD), bf16),
            pltpu.VMEM((STAGES, 2, LINE, HD), f32),
            pltpu.VMEM((STAGES, 4, LINE, HD), bf16),
            pltpu.VMEM((STAGES, 2, HALO, HD), bf16),
            pltpu.VMEM((STAGES, 2, HALO, HD), bf16),
            pltpu.VMEM((1, LINE), jnp.int32),
            sems((STAGES, 4, NX - 1)),
            sems((STAGES, 4, NX - 1)),
            sems((STAGES, 4)),
            sems((STAGES, 2)),
            sems((STAGES, 2)),
            sems((STAGES, 2)),
            sems((STAGES, 2)),
            sems((STAGES, 4, NX)),
            sems((STAGES, 4, NX)),
        ],
        compiler_params=pltpu.CompilerParams(
            collective_id=0, has_side_effects=True, vmem_limit_bytes=56 << 20
        ),
        name="attention",
    )(module_lengths.reshape(1, -1), query_in, key_in, value_in, grad_out)


def solution(mesh):
    tokens = P(("seq", "head"), None)
    n_seq, n_head = mesh.shape["seq"], mesh.shape["head"]
    return jax.shard_map(
        functools.partial(shards, n_seq, n_head // NX),
        mesh=mesh,
        in_specs=(tokens,) * 4 + (P(),),
        out_specs=(tokens,) * 4,
        check_vma=False,
    )
```

```python
import functools

import jax
import jax.numpy as jnp
from jax import lax
from jax.experimental import pallas as pl
from jax.experimental.pallas import tpu as pltpu
from jax.sharding import PartitionSpec as P

HD = 128
ROWS = 128
NX = 4
STAGES = 4
LINE = NX * ROWS
HALO = 256
SCALE = HD ** (-0.5)
LOG2E = 1.4426950408889634
MASKED = -1e30
MESH = pl.DeviceIdType.MESH


def dot(a, b, dims):
    return lax.dot_general(a, b, (dims, ((), ())), preferred_element_type=jnp.float32)


def kernel(
    n_seq,
    n_y,
    len_ref,
    q_in,
    k_in,
    v_in,
    g_in,
    o_out,
    dq_out,
    dk_out,
    dv_out,
    qg,
    kv,
    acc,
    outs,
    part_in,
    part_out,
    start_ref,
    len_held,
    len_sem,
    in_send,
    in_recv,
    own_sem,
    halo_send,
    halo_recv,
    part_send,
    part_recv,
    out_send,
    out_recv,
):
    s = lax.axis_index("seq")
    h = lax.axis_index("head")
    y, x = h // NX, h % NX
    ins = (k_in, v_in, q_in, g_in)
    results = (o_out, dq_out, dk_out, dv_out)
    is_first = (s == 0) & (y == 0)
    is_last = (s == n_seq - 1) & (y == n_y - 1)
    wrap_next = (y + 1) // n_y
    after = ((s + wrap_next) % n_seq, ((y + 1) % n_y) * NX + x)
    wrap_prev = (n_y - y) // n_y
    before = ((s + n_seq - wrap_prev) % n_seq, ((y + n_y - 1) % n_y) * NX + x)

    def in_row(peer_x):
        return (s, y * NX + peer_x)

    def rows(at):
        return pl.ds(pl.multiple_of(at * ROWS, ROWS), ROWS)

    def cols(owner, st):
        return pl.ds(pl.multiple_of((owner * STAGES + st) * HD, HD), HD)

    def landing(st, t, from_x):
        if t < 2:
            return kv.at[st, t, rows(from_x + HALO // ROWS)]
        return qg.at[st, t - 2, rows(from_x)]

    def in_copy(st, t, d):
        to = (x + d) % NX
        return pltpu.make_async_remote_copy(
            src_ref=ins[t].at[:, cols(to, st)],
            dst_ref=landing(st, t, x),
            send_sem=in_send.at[st, t, d - 1],
            recv_sem=in_recv.at[st, t, d - 1],
            device_id=in_row(to),
            device_id_type=MESH,
        )

    def own_copy(st, t):
        return pltpu.make_async_copy(
            ins[t].at[:, cols(x, st)], landing(st, t, x), own_sem.at[st, t]
        )

    def halo_copy(st, t):
        return pltpu.make_async_remote_copy(
            src_ref=kv.at[st, t, pl.ds(LINE, HALO)],
            dst_ref=kv.at[st, t, pl.ds(0, HALO)],
            send_sem=halo_send.at[st, t],
            recv_sem=halo_recv.at[st, t],
            device_id=after,
            device_id_type=MESH,
        )

    def part_copy(st, t):
        return pltpu.make_async_remote_copy(
            src_ref=part_out.at[st, t],
            dst_ref=part_in.at[st, t],
            send_sem=part_send.at[st, t],
            recv_sem=part_recv.at[st, t],
            device_id=before,
            device_id_type=MESH,
        )

    def out_copy(st, t, to):
        return pltpu.make_async_remote_copy(
            src_ref=outs.at[st, t, pl.ds(to * ROWS, ROWS)],
            dst_ref=results[t].at[:, cols(x, st)],
            send_sem=out_send.at[st, t, to],
            recv_sem=out_recv.at[st, t, x],
            device_id=in_row(to),
            device_id_type=MESH,
        )

    def out_own(st, t, to):
        return pltpu.make_async_copy(
            outs.at[st, t, pl.ds(to * ROWS, ROWS)],
            results[t].at[:, cols(x, st)],
            out_recv.at[st, t, x],
        )

    def send_out(st, kinds, half):
        for to in (2 * half, 2 * half + 1):

            @pl.when(x != to)
            def _():
                for t in kinds:
                    out_copy(st, t, to).start()

            @pl.when(x == to)
            def _():
                for t in kinds:
                    out_own(st, t, to).start()

    take_lengths = pltpu.make_async_copy(len_ref, len_held, len_sem)
    take_lengths.start()

    barrier = pltpu.get_barrier_semaphore()
    for d in range(1, NX):
        pl.semaphore_signal(barrier, inc=1, device_id=in_row((x + d) % NX), device_id_type=MESH)
    for there, missing in ((after, is_last), (before, is_first)):

        @pl.when(jnp.logical_not(missing))
        def _():
            pl.semaphore_signal(barrier, inc=1, device_id=there, device_id_type=MESH)

    row, n_rows = s * n_y + y, n_seq * n_y
    not_first = (row + n_rows - 1) // n_rows
    not_last = (2 * n_rows - 2 - row) // n_rows
    pl.semaphore_wait(barrier, NX - 1 + not_first + not_last)

    def send_in(st, carry):
        for t in range(4):
            for d in (2, 1, 3):
                in_copy(st, t, d).start()
            own_copy(st, t).start()
        return carry

    lax.fori_loop(0, STAGES, send_in, 0)

    @pl.when(is_first)
    def _():
        kv[:, :, pl.ds(0, HALO), :] = jnp.zeros((STAGES, 2, HALO, HD), kv.dtype)

    @pl.when(is_last)
    def _():
        part_in[...] = jnp.zeros_like(part_in)

    take_lengths.wait()
    lengths = len_held[...].astype(jnp.float32)
    n_mod = lengths.shape[1]
    m_at = lax.broadcasted_iota(jnp.int32, (n_mod, n_mod), 0)
    l_at = lax.broadcasted_iota(jnp.int32, (n_mod, n_mod), 1)
    ends = jnp.sum(jnp.where(l_at <= m_at, lengths, 0.0), axis=1, keepdims=True)
    base = (s * n_y + y) * LINE
    token = (base + lax.broadcasted_iota(jnp.int32, (1, LINE), 1)).astype(jnp.float32)
    begun = jnp.max(jnp.where(ends <= token, ends, 0.0), axis=0, keepdims=True)
    start_ref[...] = begun.astype(jnp.int32) - base

    def block(st, half):
        q = qg[st, 0, pl.ds(half * HALO, HALO), :]
        g = qg[st, 1, pl.ds(half * HALO, HALO), :]
        k = kv[st, 0, pl.ds(half * HALO, 2 * HALO), :]
        v = kv[st, 1, pl.ds(half * HALO, 2 * HALO), :]
        first = start_ref[:, pl.ds(half * HALO, HALO)] - half * HALO
        key_at = lax.broadcasted_iota(jnp.int32, (2 * HALO, HALO), 0) - HALO
        query_at = lax.broadcasted_iota(jnp.int32, (2 * HALO, HALO), 1)
        allowed = (key_at <= query_at) & (key_at >= first)
        scores = jnp.where(allowed, dot(k, q, ((1,), (1,))) * (SCALE * LOG2E), MASKED)
        top = jnp.max(scores, axis=0, keepdims=True)
        powers = jnp.exp2(scores - top)
        weights = powers * (1.0 / jnp.sum(powers, axis=0, keepdims=True))
        weight_bf = weights.astype(jnp.bfloat16)
        dprobs = dot(v, g, ((1,), (1,)))
        delta = jnp.sum(weights * dprobs, axis=0, keepdims=True)
        dscores = (weights * (dprobs - delta)).astype(jnp.bfloat16)
        here = pl.ds(half * HALO, HALO)
        outs[st, 0, here, :] = dot(weight_bf, v, ((0,), (0,))).astype(jnp.bfloat16)
        outs[st, 1, here, :] = (dot(dscores, k, ((0,), (0,))) * SCALE).astype(jnp.bfloat16)
        dk = dot(dscores, q, ((1,), (0,))) * SCALE
        dv = dot(weight_bf, g, ((1,), (0,)))
        return dk, dv

    def finish(st):
        @pl.when(jnp.logical_not(is_last))
        def _():
            for t in range(2):
                part_copy(st, t).wait_recv()

        for t in range(2):
            total = acc[st, t, pl.ds(HALO, HALO), :] + part_in[st, t].astype(jnp.float32)
            outs[st, 2 + t, pl.ds(HALO, HALO), :] = total.astype(jnp.bfloat16)
        send_out(st, (2, 3), 1)

    def near(st):
        for t in range(4):
            own_copy(st, t).wait()
            for d in range(1, NX):
                in_copy(st, t, d).wait_recv()

        @pl.when(jnp.logical_not(is_last))
        def _():
            for t in range(2):
                halo_copy(st, t).start()

        for t, grad in enumerate(block(st, 1)):
            acc[st, t] = grad
        send_out(st, (0, 1), 1)

    def far(st):
        @pl.when(jnp.logical_not(is_first))
        def _():
            for t in range(2):
                halo_copy(st, t).wait_recv()

        for t, grad in enumerate(block(st, 0)):
            part_out[st, t] = grad[:HALO].astype(jnp.bfloat16)
            total = acc[st, t, pl.ds(0, HALO), :] + grad[HALO:]
            outs[st, 2 + t, pl.ds(0, HALO), :] = total.astype(jnp.bfloat16)

        @pl.when(jnp.logical_not(is_first))
        def _():
            for t in range(2):
                part_copy(st, t).start()

        send_out(st, (0, 1, 2, 3), 0)

    def stage(st, carry):
        @pl.when(st < STAGES)
        def _():
            near(st)

        @pl.when((st >= 1) & (st < STAGES + 1))
        def _():
            far(st - 1)

        @pl.when(st >= 2)
        def _():
            finish(st - 2)

        return carry

    lax.fori_loop(0, STAGES + 2, stage, 0)

    def drain(st, carry):
        for t in range(4):
            for d in range(1, NX):
                in_copy(st, t, d).wait_send()

        @pl.when(jnp.logical_not(is_last))
        def _():
            for t in range(2):
                halo_copy(st, t).wait_send()

        @pl.when(jnp.logical_not(is_first))
        def _():
            for t in range(2):
                part_copy(st, t).wait_send()

        for t in range(4):
            for peer in range(NX):

                @pl.when(x != peer)
                def _():
                    out_copy(st, t, peer).wait_send()
                    pltpu.make_async_remote_copy(
                        src_ref=outs.at[st, t, pl.ds(peer * ROWS, ROWS)],
                        dst_ref=results[t].at[:, cols(peer, st)],
                        send_sem=out_send.at[st, t, peer],
                        recv_sem=out_recv.at[st, t, peer],
                        device_id=in_row(peer),
                        device_id_type=MESH,
                    ).wait_recv()

                @pl.when(x == peer)
                def _():
                    out_own(st, t, peer).wait()
        return carry

    lax.fori_loop(0, STAGES, drain, 0)


def settle(*refs):
    sems = refs[-1]
    n = len(refs) // 2
    moves = [pltpu.make_async_copy(refs[i], refs[n + i], sems.at[i]) for i in range(n)]
    for move in moves:
        move.start()
    for move in moves:
        move.wait()


def shards(n_seq, n_y, query_in, key_in, value_in, grad_out, module_lengths):
    any_space = pl.BlockSpec(memory_space=pl.ANY)
    vmem = pl.BlockSpec(memory_space=pltpu.VMEM)
    bf16, f32 = jnp.bfloat16, jnp.float32
    sems = pltpu.SemaphoreType.DMA
    small = module_lengths.reshape(1, -1)
    operands = [
        pltpu.with_memory_space_constraint(a, pltpu.HBM)
        for a in (small, query_in, key_in, value_in, grad_out)
    ]
    results = pl.pallas_call(
        functools.partial(kernel, n_seq, n_y),
        out_shape=[pltpu.VMEM(query_in.shape, bf16)] * 4,
        in_specs=[any_space] * 5,
        out_specs=[vmem] * 4,
        scratch_shapes=[
            pltpu.VMEM((STAGES, 2, LINE, HD), bf16),
            pltpu.VMEM((STAGES, 2, LINE + HALO, HD), bf16),
            pltpu.VMEM((STAGES, 2, LINE, HD), f32),
            pltpu.VMEM((STAGES, 4, LINE, HD), bf16),
            pltpu.VMEM((STAGES, 2, HALO, HD), bf16),
            pltpu.VMEM((STAGES, 2, HALO, HD), bf16),
            pltpu.VMEM((1, LINE), jnp.int32),
            pltpu.VMEM((1, module_lengths.shape[0]), jnp.int32),
            sems,
            sems((STAGES, 4, NX - 1)),
            sems((STAGES, 4, NX - 1)),
            sems((STAGES, 4)),
            sems((STAGES, 2)),
            sems((STAGES, 2)),
            sems((STAGES, 2)),
            sems((STAGES, 2)),
            sems((STAGES, 4, NX)),
            sems((STAGES, 4, NX)),
        ],
        compiler_params=pltpu.CompilerParams(
            collective_id=0, has_side_effects=True, vmem_limit_bytes=24 << 20
        ),
        name="attention",
    )(*operands)
    return pl.pallas_call(
        settle,
        out_shape=[pltpu.HBM(query_in.shape, bf16)] * 4,
        in_specs=[vmem] * 4,
        out_specs=[any_space] * 4,
        scratch_shapes=[sems((4,))],
        name="settle",
    )(*[pltpu.with_memory_space_constraint(a, pltpu.VMEM) for a in results])


def solution(mesh):
    tokens = P(("seq", "head"), None)
    n_seq, n_head = mesh.shape["seq"], mesh.shape["head"]
    return jax.shard_map(
        functools.partial(shards, n_seq, n_head // NX),
        mesh=mesh,
        in_specs=(tokens,) * 4 + (P(),),
        out_specs=(tokens,) * 4,
        check_vma=False,
    )
```

```python
import functools

import jax
import jax.numpy as jnp
from jax import lax
from jax.experimental import pallas as pl
from jax.experimental.pallas import tpu as pltpu
from jax.sharding import PartitionSpec as P

HD = 128
ROWS = 128
NX = 4
PAIRS = 2
EACH = 2
WIDE = EACH * 128
LINE = NX * ROWS
HALO = 256
SCALE = HD ** (-0.5)
LOG2E = 1.4426950408889634
MASKED = -1e30
MESH = pl.DeviceIdType.MESH


def dot(a, b, dims):
    return lax.dot_general(a, b, (dims, ((), ())), preferred_element_type=jnp.float32)


def kernel(
    n_seq,
    n_y,
    len_ref,
    q_in,
    k_in,
    v_in,
    g_in,
    o_out,
    dq_out,
    dk_out,
    dv_out,
    qg,
    kv,
    acc,
    outs,
    part_in,
    part_out,
    start_ref,
    len_held,
    len_sem,
    go,
    in_send,
    in_recv,
    own_sem,
    halo_send,
    halo_recv,
    part_send,
    part_recv,
    out_send,
    out_recv,
):
    s = lax.axis_index("seq")
    h = lax.axis_index("head")
    y, x = h // NX, h % NX
    ins = (k_in, v_in, q_in, g_in)
    results = (o_out, dq_out, dk_out, dv_out)
    is_first = (s == 0) & (y == 0)
    is_last = (s == n_seq - 1) & (y == n_y - 1)
    wrap_next = (y + 1) // n_y
    after = ((s + wrap_next) % n_seq, ((y + 1) % n_y) * NX + x)
    wrap_prev = (n_y - y) // n_y
    before = ((s + n_seq - wrap_prev) % n_seq, ((y + n_y - 1) % n_y) * NX + x)

    def in_row(peer_x):
        return (s, y * NX + peer_x)

    def rows(at):
        return pl.ds(pl.multiple_of(at * ROWS, ROWS), ROWS)

    def cols(owner, p):
        return pl.ds(pl.multiple_of((owner * PAIRS + p) * WIDE, WIDE), WIDE)

    def head(e):
        return pl.ds(e * HD, HD)

    def landing(p, t, from_x):
        if t < 2:
            return kv.at[p, t, rows(from_x + HALO // ROWS)]
        return qg.at[p, t - 2, rows(from_x)]

    def in_copy(p, t, d):
        to = (x + d) % NX
        return pltpu.make_async_remote_copy(
            src_ref=ins[t].at[:, cols(to, p)],
            dst_ref=landing(p, t, x),
            send_sem=in_send.at[p, t, d - 1],
            recv_sem=in_recv.at[p, t, d - 1],
            device_id=in_row(to),
            device_id_type=MESH,
        )

    def own_copy(p, t):
        return pltpu.make_async_copy(
            ins[t].at[:, cols(x, p)], landing(p, t, x), own_sem.at[p, t]
        )

    def halo_copy(p, e, t):
        return pltpu.make_async_remote_copy(
            src_ref=kv.at[p, t, pl.ds(LINE, HALO), head(e)],
            dst_ref=kv.at[p, t, pl.ds(0, HALO), head(e)],
            send_sem=halo_send.at[p, e, t],
            recv_sem=halo_recv.at[p, e, t],
            device_id=after,
            device_id_type=MESH,
        )

    def part_copy(p, e, t):
        return pltpu.make_async_remote_copy(
            src_ref=part_out.at[p, e, t],
            dst_ref=part_in.at[p, e, t],
            send_sem=part_send.at[p, e, t],
            recv_sem=part_recv.at[p, e, t],
            device_id=before,
            device_id_type=MESH,
        )

    def out_copy(p, t, to):
        return pltpu.make_async_remote_copy(
            src_ref=outs.at[p, t, pl.ds(to * ROWS, ROWS)],
            dst_ref=results[t].at[:, cols(x, p)],
            send_sem=out_send.at[p, t, to],
            recv_sem=out_recv.at[p, t, x],
            device_id=in_row(to),
            device_id_type=MESH,
        )

    def out_own(p, t, to):
        return pltpu.make_async_copy(
            outs.at[p, t, pl.ds(to * ROWS, ROWS)],
            results[t].at[:, cols(x, p)],
            out_recv.at[p, t, x],
        )

    def send_out(p, kinds, half):
        for to in (2 * half, 2 * half + 1):

            @pl.when(x != to)
            def _():
                for t in kinds:
                    out_copy(p, t, to).start()

            @pl.when(x == to)
            def _():
                for t in kinds:
                    out_own(p, t, to).start()

    take_lengths = pltpu.make_async_copy(len_ref, len_held, len_sem)
    take_lengths.start()

    barrier = pltpu.get_barrier_semaphore()

    @pl.when(x != 0)
    def _():
        pl.semaphore_signal(barrier, inc=1, device_id=in_row(0), device_id_type=MESH)

    @pl.when(x == 0)
    def _():
        pl.semaphore_wait(barrier, NX - 1)
        for peer in range(1, NX):
            pl.semaphore_signal(go, inc=1, device_id=in_row(peer), device_id_type=MESH)

    @pl.when(x != 0)
    def _():
        pl.semaphore_wait(go, 1)

    def greet():
        @pl.when(x != 0)
        def _():
            for there, missing in ((after, is_last), (before, is_first)):

                @pl.when(jnp.logical_not(missing))
                def _():
                    pl.semaphore_signal(barrier, inc=1, device_id=there, device_id_type=MESH)

    def greeted():
        row, n_rows = s * n_y + y, n_seq * n_y
        not_first = (row + n_rows - 1) // n_rows
        not_last = (2 * n_rows - 2 - row) // n_rows

        @pl.when(x != 0)
        def _():
            pl.semaphore_wait(barrier, not_first + not_last)

        @pl.when(x == 1)
        def _():
            pl.semaphore_signal(go, inc=1, device_id=in_row(0), device_id_type=MESH)

        @pl.when(x == 0)
        def _():
            pl.semaphore_wait(go, 1)

    def send_in(p, carry):
        for t in range(4):
            for d in (2, 1, 3):
                in_copy(p, t, d).start()
            own_copy(p, t).start()
        return carry

    greet()
    lax.fori_loop(0, PAIRS, send_in, 0)

    @pl.when(is_first)
    def _():
        kv[:, :, pl.ds(0, HALO), :] = jnp.zeros((PAIRS, 2, HALO, WIDE), kv.dtype)

    @pl.when(is_last)
    def _():
        part_in[...] = jnp.zeros_like(part_in)

    take_lengths.wait()
    lengths = len_held[...].astype(jnp.float32)
    n_mod = lengths.shape[1]
    m_at = lax.broadcasted_iota(jnp.int32, (n_mod, n_mod), 0)
    l_at = lax.broadcasted_iota(jnp.int32, (n_mod, n_mod), 1)
    ends = jnp.sum(jnp.where(l_at <= m_at, lengths, 0.0), axis=1, keepdims=True)
    base = (s * n_y + y) * LINE
    token = (base + lax.broadcasted_iota(jnp.int32, (1, LINE), 1)).astype(jnp.float32)
    begun = jnp.max(jnp.where(ends <= token, ends, 0.0), axis=0, keepdims=True)
    start_ref[...] = begun.astype(jnp.int32) - base
    greeted()

    def block(p, e, half):
        q = qg[p, 0, pl.ds(half * HALO, HALO), head(e)]
        g = qg[p, 1, pl.ds(half * HALO, HALO), head(e)]
        k = kv[p, 0, pl.ds(half * HALO, 2 * HALO), head(e)]
        v = kv[p, 1, pl.ds(half * HALO, 2 * HALO), head(e)]
        first = start_ref[:, pl.ds(half * HALO, HALO)] - half * HALO
        key_at = lax.broadcasted_iota(jnp.int32, (2 * HALO, HALO), 0) - HALO
        query_at = lax.broadcasted_iota(jnp.int32, (2 * HALO, HALO), 1)
        allowed = (key_at <= query_at) & (key_at >= first)
        scores = jnp.where(allowed, dot(k, q, ((1,), (1,))) * (SCALE * LOG2E), MASKED)
        top = jnp.max(scores, axis=0, keepdims=True)
        powers = jnp.exp2(scores - top)
        weights = powers * (1.0 / jnp.sum(powers, axis=0, keepdims=True))
        weight_bf = weights.astype(jnp.bfloat16)
        dprobs = dot(v, g, ((1,), (1,)))
        delta = jnp.sum(weights * dprobs, axis=0, keepdims=True)
        dscores = (weights * (dprobs - delta)).astype(jnp.bfloat16)
        here = pl.ds(half * HALO, HALO)
        outs[p, 0, here, head(e)] = dot(weight_bf, v, ((0,), (0,))).astype(jnp.bfloat16)
        outs[p, 1, here, head(e)] = (dot(dscores, k, ((0,), (0,))) * SCALE).astype(jnp.bfloat16)
        dk = dot(dscores, q, ((1,), (0,))) * SCALE
        dv = dot(weight_bf, g, ((1,), (0,)))
        return dk, dv

    def near(p):
        for t in range(4):
            own_copy(p, t).wait()
            for d in range(1, NX):
                in_copy(p, t, d).wait_recv()

        @pl.when(jnp.logical_not(is_last))
        def _():
            for e in range(EACH):
                for t in range(2):
                    halo_copy(p, e, t).start()

        for e in range(EACH):
            for t, grad in enumerate(block(p, e, 1)):
                acc[p, e, t] = grad
        send_out(p, (0, 1), 1)

    def far(p):
        for e in range(EACH):

            @pl.when(jnp.logical_not(is_first))
            def _():
                for t in range(2):
                    halo_copy(p, e, t).wait_recv()

            for t, grad in enumerate(block(p, e, 0)):
                part_out[p, e, t] = grad[:HALO].astype(jnp.bfloat16)
                total = acc[p, e, t, pl.ds(0, HALO), :] + grad[HALO:]
                outs[p, 2 + t, pl.ds(0, HALO), head(e)] = total.astype(jnp.bfloat16)

            @pl.when(jnp.logical_not(is_first))
            def _():
                for t in range(2):
                    part_copy(p, e, t).start()

        send_out(p, (0, 1, 2, 3), 0)

    def finish(p):
        for e in range(EACH):

            @pl.when(jnp.logical_not(is_last))
            def _():
                for t in range(2):
                    part_copy(p, e, t).wait_recv()

            for t in range(2):
                total = acc[p, e, t, pl.ds(HALO, HALO), :] + part_in[p, e, t].astype(jnp.float32)
                outs[p, 2 + t, pl.ds(HALO, HALO), head(e)] = total.astype(jnp.bfloat16)
        send_out(p, (2, 3), 1)

    def pair(p, carry):
        near(p)

        @pl.when(p > 0)
        def _():
            finish(p - 1)

        far(p)
        return carry

    lax.fori_loop(0, PAIRS, pair, 0)
    finish(PAIRS - 1)

    def drain(p, carry):
        for t in range(4):
            for d in range(1, NX):
                in_copy(p, t, d).wait_send()

        @pl.when(jnp.logical_not(is_last))
        def _():
            for e in range(EACH):
                for t in range(2):
                    halo_copy(p, e, t).wait_send()

        @pl.when(jnp.logical_not(is_first))
        def _():
            for e in range(EACH):
                for t in range(2):
                    part_copy(p, e, t).wait_send()

        for t in range(4):
            for peer in range(NX):

                @pl.when(x != peer)
                def _():
                    out_copy(p, t, peer).wait_send()
                    pltpu.make_async_remote_copy(
                        src_ref=outs.at[p, t, pl.ds(peer * ROWS, ROWS)],
                        dst_ref=results[t].at[:, cols(peer, p)],
                        send_sem=out_send.at[p, t, peer],
                        recv_sem=out_recv.at[p, t, peer],
                        device_id=in_row(peer),
                        device_id_type=MESH,
                    ).wait_recv()

                @pl.when(x == peer)
                def _():
                    out_own(p, t, peer).wait()
        return carry

    lax.fori_loop(0, PAIRS, drain, 0)


def settle(*refs):
    sems = refs[-1]
    n = len(refs) // 2
    moves = [pltpu.make_async_copy(refs[i], refs[n + i], sems.at[i]) for i in range(n)]
    for move in moves:
        move.start()
    for move in moves:
        move.wait()


def shards(n_seq, n_y, query_in, key_in, value_in, grad_out, module_lengths):
    any_space = pl.BlockSpec(memory_space=pl.ANY)
    vmem = pl.BlockSpec(memory_space=pltpu.VMEM)
    bf16, f32 = jnp.bfloat16, jnp.float32
    sems = pltpu.SemaphoreType.DMA
    small = module_lengths.reshape(1, -1)
    operands = [
        pltpu.with_memory_space_constraint(a, pltpu.HBM)
        for a in (small, query_in, key_in, value_in, grad_out)
    ]
    results = pl.pallas_call(
        functools.partial(kernel, n_seq, n_y),
        out_shape=[pltpu.VMEM(query_in.shape, bf16)] * 4,
        in_specs=[any_space] * 5,
        out_specs=[vmem] * 4,
        scratch_shapes=[
            pltpu.VMEM((PAIRS, 2, LINE, WIDE), bf16),
            pltpu.VMEM((PAIRS, 2, LINE + HALO, WIDE), bf16),
            pltpu.VMEM((PAIRS, EACH, 2, LINE, HD), f32),
            pltpu.VMEM((PAIRS, 4, LINE, WIDE), bf16),
            pltpu.VMEM((PAIRS, EACH, 2, HALO, HD), bf16),
            pltpu.VMEM((PAIRS, EACH, 2, HALO, HD), bf16),
            pltpu.VMEM((1, LINE), jnp.int32),
            pltpu.VMEM((1, module_lengths.shape[0]), jnp.int32),
            sems,
            pltpu.SemaphoreType.REGULAR,
            sems((PAIRS, 4, NX - 1)),
            sems((PAIRS, 4, NX - 1)),
            sems((PAIRS, 4)),
            sems((PAIRS, EACH, 2)),
            sems((PAIRS, EACH, 2)),
            sems((PAIRS, EACH, 2)),
            sems((PAIRS, EACH, 2)),
            sems((PAIRS, 4, NX)),
            sems((PAIRS, 4, NX)),
        ],
        compiler_params=pltpu.CompilerParams(
            collective_id=0, has_side_effects=True, vmem_limit_bytes=24 << 20
        ),
        name="attention",
    )(*operands)
    return pl.pallas_call(
        settle,
        out_shape=[pltpu.HBM(query_in.shape, bf16)] * 4,
        in_specs=[vmem] * 4,
        out_specs=[any_space] * 4,
        scratch_shapes=[sems((4,))],
        name="settle",
    )(*[pltpu.with_memory_space_constraint(a, pltpu.VMEM) for a in results])


def solution(mesh):
    tokens = P(("seq", "head"), None)
    n_seq, n_head = mesh.shape["seq"], mesh.shape["head"]
    return jax.shard_map(
        functools.partial(shards, n_seq, n_head // NX),
        mesh=mesh,
        in_specs=(tokens,) * 4 + (P(),),
        out_specs=(tokens,) * 4,
        check_vma=False,
    )
```

```python
import functools

import jax
import jax.numpy as jnp
from jax import lax
from jax.experimental import pallas as pl
from jax.experimental.pallas import tpu as pltpu
from jax.sharding import PartitionSpec as P

HD = 128
ROWS = 128
NX = 4
PAIRS = 2
EACH = 2
WIDE = EACH * 128
GREETER, RELAY = 1, 2
LINE = NX * ROWS
HALO = 256
SCALE = HD ** (-0.5)
LOG2E = 1.4426950408889634
MASKED = -1e30
MESH = pl.DeviceIdType.MESH


def dot(a, b, dims):
    return lax.dot_general(a, b, (dims, ((), ())), preferred_element_type=jnp.float32)


def kernel(
    n_seq,
    n_y,
    len_ref,
    q_in,
    k_in,
    v_in,
    g_in,
    o_out,
    dq_out,
    dk_out,
    dv_out,
    qg,
    kv,
    acc,
    outs,
    part_in,
    part_out,
    start_ref,
    len_held,
    len_sem,
    go,
    in_send,
    in_recv,
    own_sem,
    halo_send,
    halo_recv,
    part_send,
    part_recv,
    out_send,
    out_recv,
):
    s = lax.axis_index("seq")
    h = lax.axis_index("head")
    y, x = h // NX, h % NX
    ins = (k_in, v_in, q_in, g_in)
    results = (o_out, dq_out, dk_out, dv_out)
    is_first = (s == 0) & (y == 0)
    is_last = (s == n_seq - 1) & (y == n_y - 1)
    wrap_next = (y + 1) // n_y
    after = ((s + wrap_next) % n_seq, ((y + 1) % n_y) * NX + x)
    wrap_prev = (n_y - y) // n_y
    before = ((s + n_seq - wrap_prev) % n_seq, ((y + n_y - 1) % n_y) * NX + x)

    def in_row(peer_x):
        return (s, y * NX + peer_x)

    def rows(at):
        return pl.ds(pl.multiple_of(at * ROWS, ROWS), ROWS)

    def cols(owner, p):
        return pl.ds(pl.multiple_of((owner * PAIRS + p) * WIDE, WIDE), WIDE)

    def head(e):
        return pl.ds(e * HD, HD)

    def landing(p, t, from_x):
        if t < 2:
            return kv.at[p, t, rows(from_x + HALO // ROWS)]
        return qg.at[p, t - 2, rows(from_x)]

    def in_copy(p, t, d):
        to = (x + d) % NX
        return pltpu.make_async_remote_copy(
            src_ref=ins[t].at[:, cols(to, p)],
            dst_ref=landing(p, t, x),
            send_sem=in_send.at[p, t, d - 1],
            recv_sem=in_recv.at[p, t, d - 1],
            device_id=in_row(to),
            device_id_type=MESH,
        )

    def own_copy(p, t):
        return pltpu.make_async_copy(
            ins[t].at[:, cols(x, p)], landing(p, t, x), own_sem.at[p, t]
        )

    def halo_copy(p, e, t):
        return pltpu.make_async_remote_copy(
            src_ref=kv.at[p, t, pl.ds(LINE, HALO), head(e)],
            dst_ref=kv.at[p, t, pl.ds(0, HALO), head(e)],
            send_sem=halo_send.at[p, e, t],
            recv_sem=halo_recv.at[p, e, t],
            device_id=after,
            device_id_type=MESH,
        )

    def part_copy(p, e, t):
        return pltpu.make_async_remote_copy(
            src_ref=part_out.at[p, e, t],
            dst_ref=part_in.at[p, e, t],
            send_sem=part_send.at[p, e, t],
            recv_sem=part_recv.at[p, e, t],
            device_id=before,
            device_id_type=MESH,
        )

    def out_copy(p, t, to):
        return pltpu.make_async_remote_copy(
            src_ref=outs.at[p, t, pl.ds(to * ROWS, ROWS)],
            dst_ref=results[t].at[:, cols(x, p)],
            send_sem=out_send.at[p, t, to],
            recv_sem=out_recv.at[p, t, x],
            device_id=in_row(to),
            device_id_type=MESH,
        )

    def out_own(p, t, to):
        return pltpu.make_async_copy(
            outs.at[p, t, pl.ds(to * ROWS, ROWS)],
            results[t].at[:, cols(x, p)],
            out_recv.at[p, t, x],
        )

    def send_out(p, kinds, half):
        for to in (2 * half, 2 * half + 1):

            @pl.when(x != to)
            def _():
                for t in kinds:
                    out_copy(p, t, to).start()

            @pl.when(x == to)
            def _():
                for t in kinds:
                    out_own(p, t, to).start()

    take_lengths = pltpu.make_async_copy(len_ref, len_held, len_sem)
    take_lengths.start()

    barrier = pltpu.get_barrier_semaphore()
    for d in range(1, NX):
        peer = (x + d) % NX

        @pl.when(peer != GREETER)
        def _():
            pl.semaphore_signal(barrier, inc=1, device_id=in_row(peer), device_id_type=MESH)

    @pl.when(x != GREETER)
    def _():
        pl.semaphore_wait(barrier, NX - 1)

    @pl.when(x == RELAY)
    def _():
        pl.semaphore_signal(go, inc=1, device_id=in_row(GREETER), device_id_type=MESH)

    @pl.when(x == GREETER)
    def _():
        pl.semaphore_wait(go, 1)
        for there, missing in ((after, is_last), (before, is_first)):

            @pl.when(jnp.logical_not(missing))
            def _():
                pl.semaphore_signal(barrier, inc=1, device_id=there, device_id_type=MESH)

    def greeted():
        row, n_rows = s * n_y + y, n_seq * n_y
        not_first = (row + n_rows - 1) // n_rows
        not_last = (2 * n_rows - 2 - row) // n_rows

        @pl.when(x == GREETER)
        def _():
            pl.semaphore_wait(barrier, not_first + not_last)
            for d in range(1, NX):
                pl.semaphore_signal(go, inc=1, device_id=in_row((x + d) % NX), device_id_type=MESH)

        @pl.when(x != GREETER)
        def _():
            pl.semaphore_wait(go, 1)

    def send_in(p, carry):
        for t in range(4):
            for d in (2, 1, 3):
                in_copy(p, t, d).start()
            own_copy(p, t).start()
        return carry

    lax.fori_loop(0, PAIRS, send_in, 0)

    @pl.when(is_first)
    def _():
        kv[:, :, pl.ds(0, HALO), :] = jnp.zeros((PAIRS, 2, HALO, WIDE), kv.dtype)

    @pl.when(is_last)
    def _():
        part_in[...] = jnp.zeros_like(part_in)

    take_lengths.wait()
    lengths = len_held[...].astype(jnp.float32)
    n_mod = lengths.shape[1]
    m_at = lax.broadcasted_iota(jnp.int32, (n_mod, n_mod), 0)
    l_at = lax.broadcasted_iota(jnp.int32, (n_mod, n_mod), 1)
    ends = jnp.sum(jnp.where(l_at <= m_at, lengths, 0.0), axis=1, keepdims=True)
    base = (s * n_y + y) * LINE
    token = (base + lax.broadcasted_iota(jnp.int32, (1, LINE), 1)).astype(jnp.float32)
    begun = jnp.max(jnp.where(ends <= token, ends, 0.0), axis=0, keepdims=True)
    start_ref[...] = begun.astype(jnp.int32) - base
    greeted()

    def block(p, e, half):
        q = qg[p, 0, pl.ds(half * HALO, HALO), head(e)]
        g = qg[p, 1, pl.ds(half * HALO, HALO), head(e)]
        k = kv[p, 0, pl.ds(half * HALO, 2 * HALO), head(e)]
        v = kv[p, 1, pl.ds(half * HALO, 2 * HALO), head(e)]
        first = start_ref[:, pl.ds(half * HALO, HALO)] - half * HALO
        key_at = lax.broadcasted_iota(jnp.int32, (2 * HALO, HALO), 0) - HALO
        query_at = lax.broadcasted_iota(jnp.int32, (2 * HALO, HALO), 1)
        allowed = (key_at <= query_at) & (key_at >= first)
        scores = jnp.where(allowed, dot(k, q, ((1,), (1,))) * (SCALE * LOG2E), MASKED)
        top = jnp.max(scores, axis=0, keepdims=True)
        powers = jnp.exp2(scores - top)
        weights = powers * (1.0 / jnp.sum(powers, axis=0, keepdims=True))
        weight_bf = weights.astype(jnp.bfloat16)
        dprobs = dot(v, g, ((1,), (1,)))
        delta = jnp.sum(weights * dprobs, axis=0, keepdims=True)
        dscores = (weights * (dprobs - delta)).astype(jnp.bfloat16)
        here = pl.ds(half * HALO, HALO)
        outs[p, 0, here, head(e)] = dot(weight_bf, v, ((0,), (0,))).astype(jnp.bfloat16)
        outs[p, 1, here, head(e)] = (dot(dscores, k, ((0,), (0,))) * SCALE).astype(jnp.bfloat16)
        dk = dot(dscores, q, ((1,), (0,))) * SCALE
        dv = dot(weight_bf, g, ((1,), (0,)))
        return dk, dv

    def near(p):
        for t in range(4):
            own_copy(p, t).wait()
            for d in range(1, NX):
                in_copy(p, t, d).wait_recv()

        @pl.when(jnp.logical_not(is_last))
        def _():
            for e in range(EACH):
                for t in range(2):
                    halo_copy(p, e, t).start()

        for e in range(EACH):
            for t, grad in enumerate(block(p, e, 1)):
                acc[p, e, t] = grad
        send_out(p, (0, 1), 1)

    def far(p):
        for e in range(EACH):

            @pl.when(jnp.logical_not(is_first))
            def _():
                for t in range(2):
                    halo_copy(p, e, t).wait_recv()

            for t, grad in enumerate(block(p, e, 0)):
                part_out[p, e, t] = grad[:HALO].astype(jnp.bfloat16)
                total = acc[p, e, t, pl.ds(0, HALO), :] + grad[HALO:]
                outs[p, 2 + t, pl.ds(0, HALO), head(e)] = total.astype(jnp.bfloat16)

            @pl.when(jnp.logical_not(is_first))
            def _():
                for t in range(2):
                    part_copy(p, e, t).start()

        send_out(p, (0, 1, 2, 3), 0)

    def finish(p):
        for e in range(EACH):

            @pl.when(jnp.logical_not(is_last))
            def _():
                for t in range(2):
                    part_copy(p, e, t).wait_recv()

            for t in range(2):
                total = acc[p, e, t, pl.ds(HALO, HALO), :] + part_in[p, e, t].astype(jnp.float32)
                outs[p, 2 + t, pl.ds(HALO, HALO), head(e)] = total.astype(jnp.bfloat16)
        send_out(p, (2, 3), 1)

    def pair(p, carry):
        near(p)

        @pl.when(p > 0)
        def _():
            finish(p - 1)

        far(p)
        return carry

    lax.fori_loop(0, PAIRS, pair, 0)
    finish(PAIRS - 1)

    def drain(p, carry):
        for t in range(4):
            for d in range(1, NX):
                in_copy(p, t, d).wait_send()

        @pl.when(jnp.logical_not(is_last))
        def _():
            for e in range(EACH):
                for t in range(2):
                    halo_copy(p, e, t).wait_send()

        @pl.when(jnp.logical_not(is_first))
        def _():
            for e in range(EACH):
                for t in range(2):
                    part_copy(p, e, t).wait_send()

        for t in range(4):
            for peer in range(NX):

                @pl.when(x != peer)
                def _():
                    out_copy(p, t, peer).wait_send()
                    pltpu.make_async_remote_copy(
                        src_ref=outs.at[p, t, pl.ds(peer * ROWS, ROWS)],
                        dst_ref=results[t].at[:, cols(peer, p)],
                        send_sem=out_send.at[p, t, peer],
                        recv_sem=out_recv.at[p, t, peer],
                        device_id=in_row(peer),
                        device_id_type=MESH,
                    ).wait_recv()

                @pl.when(x == peer)
                def _():
                    out_own(p, t, peer).wait()
        return carry

    lax.fori_loop(0, PAIRS, drain, 0)


def settle(*refs):
    sems = refs[-1]
    n = len(refs) // 2
    moves = [pltpu.make_async_copy(refs[i], refs[n + i], sems.at[i]) for i in range(n)]
    for move in moves:
        move.start()
    for move in moves:
        move.wait()


def shards(n_seq, n_y, query_in, key_in, value_in, grad_out, module_lengths):
    any_space = pl.BlockSpec(memory_space=pl.ANY)
    vmem = pl.BlockSpec(memory_space=pltpu.VMEM)
    bf16, f32 = jnp.bfloat16, jnp.float32
    sems = pltpu.SemaphoreType.DMA
    small = module_lengths.reshape(1, -1)
    operands = [
        pltpu.with_memory_space_constraint(a, pltpu.HBM)
        for a in (small, query_in, key_in, value_in, grad_out)
    ]
    results = pl.pallas_call(
        functools.partial(kernel, n_seq, n_y),
        out_shape=[pltpu.VMEM(query_in.shape, bf16)] * 4,
        in_specs=[any_space] * 5,
        out_specs=[vmem] * 4,
        scratch_shapes=[
            pltpu.VMEM((PAIRS, 2, LINE, WIDE), bf16),
            pltpu.VMEM((PAIRS, 2, LINE + HALO, WIDE), bf16),
            pltpu.VMEM((PAIRS, EACH, 2, LINE, HD), f32),
            pltpu.VMEM((PAIRS, 4, LINE, WIDE), bf16),
            pltpu.VMEM((PAIRS, EACH, 2, HALO, HD), bf16),
            pltpu.VMEM((PAIRS, EACH, 2, HALO, HD), bf16),
            pltpu.VMEM((1, LINE), jnp.int32),
            pltpu.VMEM((1, module_lengths.shape[0]), jnp.int32),
            sems,
            pltpu.SemaphoreType.REGULAR,
            sems((PAIRS, 4, NX - 1)),
            sems((PAIRS, 4, NX - 1)),
            sems((PAIRS, 4)),
            sems((PAIRS, EACH, 2)),
            sems((PAIRS, EACH, 2)),
            sems((PAIRS, EACH, 2)),
            sems((PAIRS, EACH, 2)),
            sems((PAIRS, 4, NX)),
            sems((PAIRS, 4, NX)),
        ],
        compiler_params=pltpu.CompilerParams(
            collective_id=0, has_side_effects=True, vmem_limit_bytes=24 << 20
        ),
        name="attention",
    )(*operands)
    return pl.pallas_call(
        settle,
        out_shape=[pltpu.HBM(query_in.shape, bf16)] * 4,
        in_specs=[vmem] * 4,
        out_specs=[any_space] * 4,
        scratch_shapes=[sems((4,))],
        name="settle",
    )(*[pltpu.with_memory_space_constraint(a, pltpu.VMEM) for a in results])


def solution(mesh):
    tokens = P(("seq", "head"), None)
    n_seq, n_head = mesh.shape["seq"], mesh.shape["head"]
    return jax.shard_map(
        functools.partial(shards, n_seq, n_head // NX),
        mesh=mesh,
        in_specs=(tokens,) * 4 + (P(),),
        out_specs=(tokens,) * 4,
        check_vma=False,
    )
```

```python
import functools

import jax
import jax.numpy as jnp
from jax import lax
from jax.experimental import pallas as pl
from jax.experimental.pallas import tpu as pltpu
from jax.sharding import PartitionSpec as P

HD = 128
ROWS = 128
NX = 4
PAIRS = 2
EACH = 2
WIDE = EACH * 128
GREETER, RELAY = 1, 2
LINE = NX * ROWS
HALO = 256
SCALE = HD ** (-0.5)
LOG2E = 1.4426950408889634
MASKED = -1e30
MESH = pl.DeviceIdType.MESH


def dot(a, b, dims):
    return lax.dot_general(a, b, (dims, ((), ())), preferred_element_type=jnp.float32)


def kernel(
    n_seq,
    n_y,
    len_ref,
    q_in,
    k_in,
    v_in,
    g_in,
    results,
    land,
    acc,
    outs,
    part_in,
    part_out,
    start_ref,
    len_held,
    held,
    held_sem,
    len_sem,
    go,
    in_send,
    in_recv,
    own_sem,
    halo_send,
    halo_recv,
    part_send,
    part_recv,
    out_send,
    out_recv,
):
    s = lax.axis_index("seq")
    h = lax.axis_index("head")
    y, x = h // NX, h % NX
    ins = (k_in, v_in, q_in, g_in)
    is_first = (s == 0) & (y == 0)
    is_last = (s == n_seq - 1) & (y == n_y - 1)
    wrap_next = (y + 1) // n_y
    after = ((s + wrap_next) % n_seq, ((y + 1) % n_y) * NX + x)
    wrap_prev = (n_y - y) // n_y
    before = ((s + n_seq - wrap_prev) % n_seq, ((y + n_y - 1) % n_y) * NX + x)

    def in_row(peer_x):
        return (s, y * NX + peer_x)

    def rows(at):
        return pl.ds(pl.multiple_of(at * ROWS, ROWS), ROWS)

    def cols(owner, p):
        return pl.ds(pl.multiple_of((owner * PAIRS + p) * WIDE, WIDE), WIDE)

    def head(e):
        return pl.ds(e * HD, HD)

    def in_copy(p, d):
        to = (x + d) % NX
        return pltpu.make_async_remote_copy(
            src_ref=held.at[:, :, cols(to, p)],
            dst_ref=land.at[p, :, rows(x + HALO // ROWS)],
            send_sem=in_send.at[p, d - 1],
            recv_sem=in_recv.at[p, d - 1],
            device_id=in_row(to),
            device_id_type=MESH,
        )

    def own_copy(p):
        return pltpu.make_async_copy(
            held.at[:, :, cols(x, p)], land.at[p, :, rows(x + HALO // ROWS)], own_sem.at[p]
        )

    def halo_copy(p, e, t):
        return pltpu.make_async_remote_copy(
            src_ref=land.at[p, t, pl.ds(LINE, HALO), head(e)],
            dst_ref=land.at[p, t, pl.ds(0, HALO), head(e)],
            send_sem=halo_send.at[p, e, t],
            recv_sem=halo_recv.at[p, e, t],
            device_id=after,
            device_id_type=MESH,
        )

    def part_copy(p, e, t):
        return pltpu.make_async_remote_copy(
            src_ref=part_out.at[p, e, t],
            dst_ref=part_in.at[p, e, t],
            send_sem=part_send.at[p, e, t],
            recv_sem=part_recv.at[p, e, t],
            device_id=before,
            device_id_type=MESH,
        )

    def out_copy(p, group, kinds, to, by):
        return pltpu.make_async_remote_copy(
            src_ref=outs.at[p, kinds, pl.ds(to * ROWS, ROWS)],
            dst_ref=results.at[kinds, :, cols(by, p)],
            send_sem=out_send.at[p, group, to],
            recv_sem=out_recv.at[p, group, by],
            device_id=in_row(to),
            device_id_type=MESH,
        )

    def out_own(p, group, kinds, to):
        return pltpu.make_async_copy(
            outs.at[p, kinds, pl.ds(to * ROWS, ROWS)],
            results.at[kinds, :, cols(x, p)],
            out_recv.at[p, group, x],
        )

    groups = (((0, pl.ds(0, 4)),), ((0, pl.ds(0, 2)), (1, pl.ds(2, 2))))

    def send_out(p, half, at):
        group, kinds = groups[half][at]
        for to in (2 * half, 2 * half + 1):

            @pl.when(x != to)
            def _():
                out_copy(p, group, kinds, to, x).start()

            @pl.when(x == to)
            def _():
                out_own(p, group, kinds, to).start()

    takes = [pltpu.make_async_copy(ins[t], held.at[t], held_sem.at[t]) for t in range(4)]
    for take in takes:
        take.start()
    take_lengths = pltpu.make_async_copy(len_ref, len_held, len_sem)
    take_lengths.start()

    barrier = pltpu.get_barrier_semaphore()
    for d in range(1, NX):
        peer = (x + d) % NX

        @pl.when(peer != GREETER)
        def _():
            pl.semaphore_signal(barrier, inc=1, device_id=in_row(peer), device_id_type=MESH)

    @pl.when(x != GREETER)
    def _():
        pl.semaphore_wait(barrier, NX - 1)

    @pl.when(x == RELAY)
    def _():
        pl.semaphore_signal(go, inc=1, device_id=in_row(GREETER), device_id_type=MESH)

    @pl.when(x == GREETER)
    def _():
        pl.semaphore_wait(go, 1)
        for there, missing in ((after, is_last), (before, is_first)):

            @pl.when(jnp.logical_not(missing))
            def _():
                pl.semaphore_signal(barrier, inc=1, device_id=there, device_id_type=MESH)

    def greeted():
        row, n_rows = s * n_y + y, n_seq * n_y
        not_first = (row + n_rows - 1) // n_rows
        not_last = (2 * n_rows - 2 - row) // n_rows

        @pl.when(x == GREETER)
        def _():
            pl.semaphore_wait(barrier, not_first + not_last)
            for d in range(1, NX):
                pl.semaphore_signal(go, inc=1, device_id=in_row((x + d) % NX), device_id_type=MESH)

        @pl.when(x != GREETER)
        def _():
            pl.semaphore_wait(go, 1)

    def send_in(p, carry):
        for d in (2, 1, 3):
            in_copy(p, d).start()
        own_copy(p).start()
        return carry

    for take in takes:
        take.wait()
    lax.fori_loop(0, PAIRS, send_in, 0)

    @pl.when(is_first)
    def _():
        land[:, pl.ds(0, 2), pl.ds(0, HALO), :] = jnp.zeros((PAIRS, 2, HALO, WIDE), land.dtype)

    @pl.when(is_last)
    def _():
        part_in[...] = jnp.zeros_like(part_in)

    take_lengths.wait()
    lengths = len_held[...].astype(jnp.float32)
    n_mod = lengths.shape[1]
    m_at = lax.broadcasted_iota(jnp.int32, (n_mod, n_mod), 0)
    l_at = lax.broadcasted_iota(jnp.int32, (n_mod, n_mod), 1)
    ends = jnp.sum(jnp.where(l_at <= m_at, lengths, 0.0), axis=1, keepdims=True)
    base = (s * n_y + y) * LINE
    token = (base + lax.broadcasted_iota(jnp.int32, (1, LINE), 1)).astype(jnp.float32)
    begun = jnp.max(jnp.where(ends <= token, ends, 0.0), axis=0, keepdims=True)
    start_ref[...] = begun.astype(jnp.int32) - base
    greeted()

    def block(p, e, half):
        q = land[p, 2, pl.ds((half + 1) * HALO, HALO), head(e)]
        g = land[p, 3, pl.ds((half + 1) * HALO, HALO), head(e)]
        k = land[p, 0, pl.ds(half * HALO, 2 * HALO), head(e)]
        v = land[p, 1, pl.ds(half * HALO, 2 * HALO), head(e)]
        first = start_ref[:, pl.ds(half * HALO, HALO)] - half * HALO
        key_at = lax.broadcasted_iota(jnp.int32, (2 * HALO, HALO), 0) - HALO
        query_at = lax.broadcasted_iota(jnp.int32, (2 * HALO, HALO), 1)
        allowed = (key_at <= query_at) & (key_at >= first)
        scores = jnp.where(allowed, dot(k, q, ((1,), (1,))) * (SCALE * LOG2E), MASKED)
        top = jnp.max(scores, axis=0, keepdims=True)
        powers = jnp.exp2(scores - top)
        weights = powers * (1.0 / jnp.sum(powers, axis=0, keepdims=True))
        weight_bf = weights.astype(jnp.bfloat16)
        dprobs = dot(v, g, ((1,), (1,)))
        delta = jnp.sum(weights * dprobs, axis=0, keepdims=True)
        dscores = (weights * (dprobs - delta)).astype(jnp.bfloat16)
        here = pl.ds(half * HALO, HALO)
        outs[p, 0, here, head(e)] = dot(weight_bf, v, ((0,), (0,))).astype(jnp.bfloat16)
        outs[p, 1, here, head(e)] = (dot(dscores, k, ((0,), (0,))) * SCALE).astype(jnp.bfloat16)
        dk = dot(dscores, q, ((1,), (0,))) * SCALE
        dv = dot(weight_bf, g, ((1,), (0,)))
        return dk, dv

    def near(p):
        own_copy(p).wait()
        for d in range(1, NX):
            in_copy(p, d).wait_recv()

        @pl.when(jnp.logical_not(is_last))
        def _():
            for e in range(EACH):
                for t in range(2):
                    halo_copy(p, e, t).start()

        for e in range(EACH):
            for t, grad in enumerate(block(p, e, 1)):
                acc[p, e, t] = grad
        send_out(p, 1, 0)

    def far(p):
        for e in range(EACH):

            @pl.when(jnp.logical_not(is_first))
            def _():
                for t in range(2):
                    halo_copy(p, e, t).wait_recv()

            for t, grad in enumerate(block(p, e, 0)):
                part_out[p, e, t] = grad[:HALO].astype(jnp.bfloat16)
                total = acc[p, e, t, pl.ds(0, HALO), :] + grad[HALO:]
                outs[p, 2 + t, pl.ds(0, HALO), head(e)] = total.astype(jnp.bfloat16)

            @pl.when(jnp.logical_not(is_first))
            def _():
                for t in range(2):
                    part_copy(p, e, t).start()

        send_out(p, 0, 0)

    def finish(p):
        for e in range(EACH):

            @pl.when(jnp.logical_not(is_last))
            def _():
                for t in range(2):
                    part_copy(p, e, t).wait_recv()

            for t in range(2):
                total = acc[p, e, t, pl.ds(HALO, HALO), :] + part_in[p, e, t].astype(jnp.float32)
                outs[p, 2 + t, pl.ds(HALO, HALO), head(e)] = total.astype(jnp.bfloat16)
        send_out(p, 1, 1)

    def pair(p, carry):
        near(p)

        @pl.when(p > 0)
        def _():
            finish(p - 1)

        far(p)
        return carry

    lax.fori_loop(0, PAIRS, pair, 0)
    finish(PAIRS - 1)

    def drain(p, carry):
        for d in range(1, NX):
            in_copy(p, d).wait_send()

        @pl.when(jnp.logical_not(is_last))
        def _():
            for e in range(EACH):
                for t in range(2):
                    halo_copy(p, e, t).wait_send()

        @pl.when(jnp.logical_not(is_first))
        def _():
            for e in range(EACH):
                for t in range(2):
                    part_copy(p, e, t).wait_send()

        for half in range(2):
            for group, kinds in groups[half]:
                for to in (2 * half, 2 * half + 1):

                    @pl.when(x != to)
                    def _():
                        out_copy(p, group, kinds, to, x).wait_send()

                    @pl.when(x == to)
                    def _():
                        out_own(p, group, kinds, to).wait()
                        for by in range(NX):
                            if by != to:
                                out_copy(p, group, kinds, to, by).wait_recv()
        return carry

    lax.fori_loop(0, PAIRS, drain, 0)


def settle(results, o_out, dq_out, dk_out, dv_out, sems):
    moves = [
        pltpu.make_async_copy(results.at[t], out, sems.at[t])
        for t, out in enumerate((o_out, dq_out, dk_out, dv_out))
    ]
    for move in moves:
        move.start()
    for move in moves:
        move.wait()


def shards(n_seq, n_y, query_in, key_in, value_in, grad_out, module_lengths):
    any_space = pl.BlockSpec(memory_space=pl.ANY)
    vmem = pl.BlockSpec(memory_space=pltpu.VMEM)
    bf16, f32 = jnp.bfloat16, jnp.float32
    sems = pltpu.SemaphoreType.DMA
    small = module_lengths.reshape(1, -1)
    operands = [
        pltpu.with_memory_space_constraint(a, pltpu.HBM)
        for a in (small, query_in, key_in, value_in, grad_out)
    ]
    results = pl.pallas_call(
        functools.partial(kernel, n_seq, n_y),
        out_shape=pltpu.VMEM((4, *query_in.shape), bf16),
        in_specs=[any_space] * 5,
        out_specs=vmem,
        scratch_shapes=[
            pltpu.VMEM((PAIRS, 4, LINE + HALO, WIDE), bf16),
            pltpu.VMEM((PAIRS, EACH, 2, LINE, HD), f32),
            pltpu.VMEM((PAIRS, 4, LINE, WIDE), bf16),
            pltpu.VMEM((PAIRS, EACH, 2, HALO, HD), bf16),
            pltpu.VMEM((PAIRS, EACH, 2, HALO, HD), bf16),
            pltpu.VMEM((1, LINE), jnp.int32),
            pltpu.VMEM((1, module_lengths.shape[0]), jnp.int32),
            pltpu.VMEM((4, *query_in.shape), bf16),
            sems((4,)),
            sems,
            pltpu.SemaphoreType.REGULAR,
            sems((PAIRS, NX - 1)),
            sems((PAIRS, NX - 1)),
            sems((PAIRS,)),
            sems((PAIRS, EACH, 2)),
            sems((PAIRS, EACH, 2)),
            sems((PAIRS, EACH, 2)),
            sems((PAIRS, EACH, 2)),
            sems((PAIRS, 2, NX)),
            sems((PAIRS, 2, NX)),
        ],
        compiler_params=pltpu.CompilerParams(
            collective_id=0, has_side_effects=True, vmem_limit_bytes=24 << 20
        ),
        name="attention",
    )(*operands)
    return pl.pallas_call(
        settle,
        out_shape=[pltpu.HBM(query_in.shape, bf16)] * 4,
        in_specs=[vmem],
        out_specs=[any_space] * 4,
        scratch_shapes=[sems((4,))],
        name="settle",
    )(pltpu.with_memory_space_constraint(results, pltpu.VMEM))


def solution(mesh):
    tokens = P(("seq", "head"), None)
    n_seq, n_head = mesh.shape["seq"], mesh.shape["head"]
    return jax.shard_map(
        functools.partial(shards, n_seq, n_head // NX),
        mesh=mesh,
        in_specs=(tokens,) * 4 + (P(),),
        out_specs=(tokens,) * 4,
        check_vma=False,
    )
```

```python
import functools

import jax
import jax.numpy as jnp
from jax import lax
from jax.experimental import pallas as pl
from jax.experimental.pallas import tpu as pltpu
from jax.sharding import PartitionSpec as P

HD = 128
ROWS = 128
NX = 4
PAIRS = 4
EACH = 1
WIDE = EACH * 128
GREETER, RELAY = 1, 2
LINE = NX * ROWS
HALO = 256
SCALE = HD ** (-0.5)
LOG2E = 1.4426950408889634
MASKED = -1e30
MESH = pl.DeviceIdType.MESH


def dot(a, b, dims):
    return lax.dot_general(a, b, (dims, ((), ())), preferred_element_type=jnp.float32)


def kernel(
    n_seq,
    n_y,
    len_ref,
    q_in,
    k_in,
    v_in,
    g_in,
    results,
    land,
    acc,
    outs,
    part_in,
    part_out,
    start_ref,
    len_held,
    held,
    held_sem,
    len_sem,
    go,
    in_send,
    in_recv,
    own_sem,
    halo_send,
    halo_recv,
    part_send,
    part_recv,
    out_send,
    out_recv,
):
    s = lax.axis_index("seq")
    h = lax.axis_index("head")
    y, x = h // NX, h % NX
    ins = (k_in, v_in, q_in, g_in)
    is_first = (s == 0) & (y == 0)
    is_last = (s == n_seq - 1) & (y == n_y - 1)
    wrap_next = (y + 1) // n_y
    after = ((s + wrap_next) % n_seq, ((y + 1) % n_y) * NX + x)
    wrap_prev = (n_y - y) // n_y
    before = ((s + n_seq - wrap_prev) % n_seq, ((y + n_y - 1) % n_y) * NX + x)

    def in_row(peer_x):
        return (s, y * NX + peer_x)

    def rows(at):
        return pl.ds(pl.multiple_of(at * ROWS, ROWS), ROWS)

    def cols(owner, p):
        return pl.ds(pl.multiple_of((owner * PAIRS + p) * WIDE, WIDE), WIDE)

    def head(e):
        return pl.ds(e * HD, HD)

    def in_copy(p, d):
        to = (x + d) % NX
        return pltpu.make_async_remote_copy(
            src_ref=held.at[:, :, cols(to, p)],
            dst_ref=land.at[p, :, rows(x + HALO // ROWS)],
            send_sem=in_send.at[p, d - 1],
            recv_sem=in_recv.at[p, d - 1],
            device_id=in_row(to),
            device_id_type=MESH,
        )

    def own_copy(p):
        return pltpu.make_async_copy(
            held.at[:, :, cols(x, p)], land.at[p, :, rows(x + HALO // ROWS)], own_sem.at[p]
        )

    def halo_copy(p, e, t):
        return pltpu.make_async_remote_copy(
            src_ref=land.at[p, t, pl.ds(LINE, HALO), head(e)],
            dst_ref=land.at[p, t, pl.ds(0, HALO), head(e)],
            send_sem=halo_send.at[p, e, t],
            recv_sem=halo_recv.at[p, e, t],
            device_id=after,
            device_id_type=MESH,
        )

    def part_copy(p, e, t):
        return pltpu.make_async_remote_copy(
            src_ref=part_out.at[p, e, t],
            dst_ref=part_in.at[p, e, t],
            send_sem=part_send.at[p, e, t],
            recv_sem=part_recv.at[p, e, t],
            device_id=before,
            device_id_type=MESH,
        )

    def out_copy(p, group, kinds, to, by):
        return pltpu.make_async_remote_copy(
            src_ref=outs.at[p, kinds, pl.ds(to * ROWS, ROWS)],
            dst_ref=results.at[kinds, :, cols(by, p)],
            send_sem=out_send.at[p, group, to],
            recv_sem=out_recv.at[p, group, by],
            device_id=in_row(to),
            device_id_type=MESH,
        )

    def out_own(p, group, kinds, to):
        return pltpu.make_async_copy(
            outs.at[p, kinds, pl.ds(to * ROWS, ROWS)],
            results.at[kinds, :, cols(x, p)],
            out_recv.at[p, group, x],
        )

    groups = (((0, pl.ds(0, 4)),), ((0, pl.ds(0, 2)), (1, pl.ds(2, 2))))

    def send_out(p, half, at):
        group, kinds = groups[half][at]
        for to in (2 * half, 2 * half + 1):

            @pl.when(x != to)
            def _():
                out_copy(p, group, kinds, to, x).start()

            @pl.when(x == to)
            def _():
                out_own(p, group, kinds, to).start()

    takes = [pltpu.make_async_copy(ins[t], held.at[t], held_sem.at[t]) for t in range(4)]
    for take in takes:
        take.start()
    take_lengths = pltpu.make_async_copy(len_ref, len_held, len_sem)
    take_lengths.start()

    barrier = pltpu.get_barrier_semaphore()
    for d in range(1, NX):
        peer = (x + d) % NX

        @pl.when(peer != GREETER)
        def _():
            pl.semaphore_signal(barrier, inc=1, device_id=in_row(peer), device_id_type=MESH)

    @pl.when(x != GREETER)
    def _():
        pl.semaphore_wait(barrier, NX - 1)

    @pl.when(x == RELAY)
    def _():
        pl.semaphore_signal(go, inc=1, device_id=in_row(GREETER), device_id_type=MESH)

    @pl.when(x == GREETER)
    def _():
        pl.semaphore_wait(go, 1)
        for there, missing in ((after, is_last), (before, is_first)):

            @pl.when(jnp.logical_not(missing))
            def _():
                pl.semaphore_signal(barrier, inc=1, device_id=there, device_id_type=MESH)

    def greeted():
        row, n_rows = s * n_y + y, n_seq * n_y
        not_first = (row + n_rows - 1) // n_rows
        not_last = (2 * n_rows - 2 - row) // n_rows

        @pl.when(x == GREETER)
        def _():
            pl.semaphore_wait(barrier, not_first + not_last)
            for d in range(1, NX):
                pl.semaphore_signal(go, inc=1, device_id=in_row((x + d) % NX), device_id_type=MESH)

        @pl.when(x != GREETER)
        def _():
            pl.semaphore_wait(go, 1)

    def send_in(p, carry):
        for d in (2, 1, 3):
            in_copy(p, d).start()
        own_copy(p).start()
        return carry

    for take in takes:
        take.wait()
    lax.fori_loop(0, PAIRS, send_in, 0)

    @pl.when(is_first)
    def _():
        land[:, pl.ds(0, 2), pl.ds(0, HALO), :] = jnp.zeros((PAIRS, 2, HALO, WIDE), land.dtype)

    @pl.when(is_last)
    def _():
        part_in[...] = jnp.zeros_like(part_in)

    take_lengths.wait()
    lengths = len_held[...].astype(jnp.float32)
    n_mod = lengths.shape[1]
    m_at = lax.broadcasted_iota(jnp.int32, (n_mod, n_mod), 0)
    l_at = lax.broadcasted_iota(jnp.int32, (n_mod, n_mod), 1)
    ends = jnp.sum(jnp.where(l_at <= m_at, lengths, 0.0), axis=1, keepdims=True)
    base = (s * n_y + y) * LINE
    token = (base + lax.broadcasted_iota(jnp.int32, (1, LINE), 1)).astype(jnp.float32)
    begun = jnp.max(jnp.where(ends <= token, ends, 0.0), axis=0, keepdims=True)
    start_ref[...] = begun.astype(jnp.int32) - base
    greeted()

    def block(p, e, half):
        q = land[p, 2, pl.ds((half + 1) * HALO, HALO), head(e)]
        g = land[p, 3, pl.ds((half + 1) * HALO, HALO), head(e)]
        k = land[p, 0, pl.ds(half * HALO, 2 * HALO), head(e)]
        v = land[p, 1, pl.ds(half * HALO, 2 * HALO), head(e)]
        first = start_ref[:, pl.ds(half * HALO, HALO)] - half * HALO
        key_at = lax.broadcasted_iota(jnp.int32, (2 * HALO, HALO), 0) - HALO
        query_at = lax.broadcasted_iota(jnp.int32, (2 * HALO, HALO), 1)
        allowed = (key_at <= query_at) & (key_at >= first)
        scores = jnp.where(allowed, dot(k, q, ((1,), (1,))) * (SCALE * LOG2E), MASKED)
        top = jnp.max(scores, axis=0, keepdims=True)
        powers = jnp.exp2(scores - top)
        weights = powers * (1.0 / jnp.sum(powers, axis=0, keepdims=True))
        weight_bf = weights.astype(jnp.bfloat16)
        dprobs = dot(v, g, ((1,), (1,)))
        delta = jnp.sum(weights * dprobs, axis=0, keepdims=True)
        dscores = (weights * (dprobs - delta)).astype(jnp.bfloat16)
        here = pl.ds(half * HALO, HALO)
        outs[p, 0, here, head(e)] = dot(weight_bf, v, ((0,), (0,))).astype(jnp.bfloat16)
        outs[p, 1, here, head(e)] = (dot(dscores, k, ((0,), (0,))) * SCALE).astype(jnp.bfloat16)
        dk = dot(dscores, q, ((1,), (0,))) * SCALE
        dv = dot(weight_bf, g, ((1,), (0,)))
        return dk, dv

    def near(p):
        own_copy(p).wait()
        for d in range(1, NX):
            in_copy(p, d).wait_recv()

        @pl.when(jnp.logical_not(is_last))
        def _():
            for e in range(EACH):
                for t in range(2):
                    halo_copy(p, e, t).start()

        for e in range(EACH):
            for t, grad in enumerate(block(p, e, 1)):
                acc[p, e, t] = grad
        send_out(p, 1, 0)

    def far(p):
        for e in range(EACH):

            @pl.when(jnp.logical_not(is_first))
            def _():
                for t in range(2):
                    halo_copy(p, e, t).wait_recv()

            for t, grad in enumerate(block(p, e, 0)):
                part_out[p, e, t] = grad[:HALO].astype(jnp.bfloat16)
                total = acc[p, e, t, pl.ds(0, HALO), :] + grad[HALO:]
                outs[p, 2 + t, pl.ds(0, HALO), head(e)] = total.astype(jnp.bfloat16)

            @pl.when(jnp.logical_not(is_first))
            def _():
                for t in range(2):
                    part_copy(p, e, t).start()

        send_out(p, 0, 0)

    def finish(p):
        for e in range(EACH):

            @pl.when(jnp.logical_not(is_last))
            def _():
                for t in range(2):
                    part_copy(p, e, t).wait_recv()

            for t in range(2):
                total = acc[p, e, t, pl.ds(HALO, HALO), :] + part_in[p, e, t].astype(jnp.float32)
                outs[p, 2 + t, pl.ds(HALO, HALO), head(e)] = total.astype(jnp.bfloat16)
        send_out(p, 1, 1)

    def pair(p, carry):
        near(p)

        @pl.when(p > 0)
        def _():
            finish(p - 1)

        far(p)
        return carry

    lax.fori_loop(0, PAIRS, pair, 0)
    finish(PAIRS - 1)

    def drain(p, carry):
        for d in range(1, NX):
            in_copy(p, d).wait_send()

        @pl.when(jnp.logical_not(is_last))
        def _():
            for e in range(EACH):
                for t in range(2):
                    halo_copy(p, e, t).wait_send()

        @pl.when(jnp.logical_not(is_first))
        def _():
            for e in range(EACH):
                for t in range(2):
                    part_copy(p, e, t).wait_send()

        for half in range(2):
            for group, kinds in groups[half]:
                for to in (2 * half, 2 * half + 1):

                    @pl.when(x != to)
                    def _():
                        out_copy(p, group, kinds, to, x).wait_send()

                    @pl.when(x == to)
                    def _():
                        out_own(p, group, kinds, to).wait()
                        for by in range(NX):
                            if by != to:
                                out_copy(p, group, kinds, to, by).wait_recv()
        return carry

    lax.fori_loop(0, PAIRS, drain, 0)


def settle(results, o_out, dq_out, dk_out, dv_out, sems):
    moves = [
        pltpu.make_async_copy(results.at[t], out, sems.at[t])
        for t, out in enumerate((o_out, dq_out, dk_out, dv_out))
    ]
    for move in moves:
        move.start()
    for move in moves:
        move.wait()


def shards(n_seq, n_y, query_in, key_in, value_in, grad_out, module_lengths):
    any_space = pl.BlockSpec(memory_space=pl.ANY)
    vmem = pl.BlockSpec(memory_space=pltpu.VMEM)
    bf16, f32 = jnp.bfloat16, jnp.float32
    sems = pltpu.SemaphoreType.DMA
    small = module_lengths.reshape(1, -1)
    operands = [
        pltpu.with_memory_space_constraint(a, pltpu.HBM)
        for a in (small, query_in, key_in, value_in, grad_out)
    ]
    results = pl.pallas_call(
        functools.partial(kernel, n_seq, n_y),
        out_shape=pltpu.VMEM((4, *query_in.shape), bf16),
        in_specs=[any_space] * 5,
        out_specs=vmem,
        scratch_shapes=[
            pltpu.VMEM((PAIRS, 4, LINE + HALO, WIDE), bf16),
            pltpu.VMEM((PAIRS, EACH, 2, LINE, HD), f32),
            pltpu.VMEM((PAIRS, 4, LINE, WIDE), bf16),
            pltpu.VMEM((PAIRS, EACH, 2, HALO, HD), bf16),
            pltpu.VMEM((PAIRS, EACH, 2, HALO, HD), bf16),
            pltpu.VMEM((1, LINE), jnp.int32),
            pltpu.VMEM((1, module_lengths.shape[0]), jnp.int32),
            pltpu.VMEM((4, *query_in.shape), bf16),
            sems((4,)),
            sems,
            pltpu.SemaphoreType.REGULAR,
            sems((PAIRS, NX - 1)),
            sems((PAIRS, NX - 1)),
            sems((PAIRS,)),
            sems((PAIRS, EACH, 2)),
            sems((PAIRS, EACH, 2)),
            sems((PAIRS, EACH, 2)),
            sems((PAIRS, EACH, 2)),
            sems((PAIRS, 2, NX)),
            sems((PAIRS, 2, NX)),
        ],
        compiler_params=pltpu.CompilerParams(
            collective_id=0, has_side_effects=True, vmem_limit_bytes=24 << 20
        ),
        name="attention",
    )(*operands)
    return pl.pallas_call(
        settle,
        out_shape=[pltpu.HBM(query_in.shape, bf16)] * 4,
        in_specs=[vmem],
        out_specs=[any_space] * 4,
        scratch_shapes=[sems((4,))],
        name="settle",
    )(pltpu.with_memory_space_constraint(results, pltpu.VMEM))


def solution(mesh):
    tokens = P(("seq", "head"), None)
    n_seq, n_head = mesh.shape["seq"], mesh.shape["head"]
    return jax.shard_map(
        functools.partial(shards, n_seq, n_head // NX),
        mesh=mesh,
        in_specs=(tokens,) * 4 + (P(),),
        out_specs=(tokens,) * 4,
        check_vma=False,
    )
```
